32 devices in a mesh: dp: 4 (over z), grp: 2 (over y), wid: 4 (over x, core).
Axes of the slice: x: 2, y: 2, z: 4, core: 2. Of those that a mesh axis runs over, the one named last changes fastest.
Arguments:
- hidden_in: bfloat16 [4, 1024, 896], P('dp', None, 'wid'), may hold values from -26 to 26
- doc_ids: int32 [4, 1024], P('dp'), may hold values from 0 to 4, as said below
- qkv_weight: bfloat16 [2, 896, 1152], P(None, 'wid', 'grp'), may hold values from -0.1875 to 0.1875
- qkv_bias: float32 [2, 1152], P(None, 'grp'), may hold values from -3 to 3
- out_weight: bfloat16 [2, 896, 896], P(None, 'grp', 'wid'), may hold values from -1 to 1
- gate_up: bfloat16 [2, 896, 2, 4864], P(None, 'wid', None, 'grp'), may hold values from -0.1875 to 0.1875
- down_weight: bfloat16 [2, 4864, 896], P(None, 'grp', 'wid'), may hold values from -0.078125 to 0.078125
- norm_gains: float32 [2, 2, 896], P(None, None, 'wid'), may hold values from 0.25 to 1.75
- cotangent: bfloat16 [4, 1024, 896], P('dp', None, 'wid'), may hold values from -6 to 6
Outputs:
- hidden_out: bfloat16 [4, 1024, 896], P('dp', None, 'wid')
- input_grad: float32 [4, 1024, 896], P('dp', None, 'wid')
- qkv_weight_grad: float32 [2, 896, 1152], P(None, ('wid', 'dp'), 'grp')
- qkv_bias_grad: float32 [2, 1152], P(None, ('grp', 'dp'))
- out_weight_grad: float32 [2, 896, 896], P(None, ('grp', 'dp'), 'wid')
- gate_up_grad: float32 [2, 896, 2, 4864], P(None, ('wid', 'dp'), None, 'grp')
- down_weight_grad: float32 [2, 4864, 896], P(None, ('grp', 'dp'), 'wid')
- norm_gains_grad: float32 [2, 2, 896], P(None, None, ('wid', 'dp'))
The draws below stay inside these ranges and needn't reach their ends.
Inputs may be any that keep to these rules, and one draw needn't show every extreme that they name: `doc_ids`: document numbers start at 0 in each sequence and never fall along it; every sequence holds five documents.
All inputs are finite; a program needn't handle non-finite values.
Results may differ from the reference program's by a relative error of at most 0.039.
Values may be sent and summed in bfloat16 or wider, within the bound.
A program may use at most 192 MiB of HBM per device.

```python
import math
import jax
import jax.numpy as jnp
from jax import lax

D = 896
HEADS = 14
KV_HEADS = 2
HEAD_DIM = 64
FF = 4864
LAYERS = 2
LENGTH = 1024
SEQS = 4


def draw_hidden_in(key, part):
    key = jax.random.fold_in(key, 11)
    key_rows, key_cols, key_base = jax.random.split(key, 3)
    column_norm = math.sqrt(99.0 / (2.0 * math.log(10.0)))
    column_scale = jnp.exp(jax.random.uniform(key_cols, (1, 1, D), jnp.float32, 0.0, math.log(10.0))) / column_norm
    row_scale = jnp.exp(jax.random.uniform(key_rows, (SEQS, LENGTH, 1), jnp.float32, math.log(0.3), math.log(3.0)))
    base = jax.random.truncated_normal(key_base, -4.0, 4.0, (SEQS, LENGTH, D), jnp.float32)
    return (base * row_scale * column_scale).astype(jnp.bfloat16)


def draw_doc_ids(key, part):
    key = jax.random.fold_in(key, 7)
    key_start, key_end = jax.random.split(key, 2)
    position_grid = lax.broadcasted_iota(jnp.int32, (SEQS, LENGTH), 1)
    first_cut = jax.random.randint(key_start, (SEQS, 1), 2, LENGTH // 8 + 1)
    last_cut = jax.random.randint(key_end, (SEQS, 1), LENGTH - LENGTH // 8, LENGTH - 1)
    early_cut = first_cut // 2
    tail_cut = last_cut + (LENGTH - last_cut) // 2
    boundary = (position_grid == early_cut) | (position_grid == first_cut) | (position_grid == last_cut) | (position_grid == tail_cut)
    return jnp.cumsum(boundary.astype(jnp.int32), axis=1)


def shard_levels(stream_key, shape, pieces, least, high):
    factor_of, own = 1.0, jax.random.fold_in(stream_key, 6)
    for axis_at, parts in pieces:
        steps = jnp.exp(jax.random.uniform(jax.random.fold_in(own, axis_at), (parts,), jnp.float32, least / len(pieces), high / len(pieces)))
        factor_of = factor_of * jnp.repeat(steps, shape[axis_at] // parts).reshape([-1 if axis == axis_at else 1 for axis in range(len(shape))])
    return factor_of


def bell_draw(own_key, dims, deviation, limit, shards=(), kind=jnp.bfloat16):
    array = jax.random.normal(own_key, dims, jnp.float32) * deviation
    if len(shards) > 0:
        array = shard_levels(own_key, dims, shards, -0.22, 0.18) * array
    return jnp.clip(array, min=-limit, max=limit).astype(kind)


def setup_inputs(seed: int = 0) -> dict:
    key_of = jax.random.split(jax.random.key(seed), 10)
    hidden_in = draw_hidden_in(jax.random.fold_in(key_of[9], 71), 0)
    doc_ids = draw_doc_ids(jax.random.fold_in(key_of[9], 71), 0)
    qkv_weight = bell_draw(key_of[2], (LAYERS, D, KV_HEADS * (HEADS // KV_HEADS + 2) * HEAD_DIM), D ** -0.5, 0.1875, ((1, 4), (2, 2)))
    qkv_bias = bell_draw(key_of[3], (LAYERS, KV_HEADS * (HEADS // KV_HEADS + 2) * HEAD_DIM), 0.5, 3.0, ((1, 2),), jnp.float32)
    out_weight = bell_draw(key_of[4], (LAYERS, HEADS * HEAD_DIM, D), (HEAD_DIM // 2) ** -0.5, 1.0, ((1, 2), (2, 4)))
    gate_up = bell_draw(key_of[5], (LAYERS, D, 2, FF), D ** -0.5, 0.1875, ((1, 4), (3, 2)))
    down_weight = bell_draw(key_of[6], (LAYERS, FF, D), FF ** -0.5, 0.078125, ((1, 2), (2, 4)))
    norm_gains = jnp.clip(1.0 + 0.15 * jax.random.normal(key_of[7], (LAYERS, 2, D), jnp.float32), 0.25, 1.75)
    cotangent = bell_draw(key_of[8], (SEQS, LENGTH, D), 1.0, 6.0, ((0, 4), (2, 4)))
    return {"hidden_in": hidden_in, "doc_ids": doc_ids, "qkv_weight": qkv_weight, "qkv_bias": qkv_bias, "out_weight": out_weight, "gate_up": gate_up, "down_weight": down_weight, "norm_gains": norm_gains, "cotangent": cotangent}


EPSILON = 1e-06
ROPE_BASE = 1000000.0
NEGATIVE = -1e+30
HIGHEST = lax.Precision.HIGHEST

@jax.custom_vjp
def low(v):
    return lax.optimization_barrier(v.astype(jnp.bfloat16)).astype(jnp.float32)

@jax.custom_vjp
def low_back(v):
    return v

def low_keep(v):
    return (low(v), None)

def low_pass(kept, grad):
    return (grad,)

def back_keep(v):
    return (v, None)

def back_low(kept, grad):
    return (low(grad),)
low.defvjp(low_keep, low_pass)
low_back.defvjp(back_keep, back_low)

def rope_tables(doc_ids):
    position_grid = lax.broadcasted_iota(jnp.int32, doc_ids.shape, 1)
    change = jnp.concatenate([jnp.ones_like(doc_ids[:, :1]), (doc_ids[:, 1:] != doc_ids[:, :-1]).astype(jnp.int32)], axis=1)
    starts = lax.cummax(jnp.where(change > 0, position_grid, 0), axis=1)
    places = (position_grid - starts).astype(jnp.float32)
    frequency = ROPE_BASE ** (-jnp.arange(HEAD_DIM // 2, dtype=jnp.float32) / (HEAD_DIM // 2))
    angles = places[:, :, None] * frequency
    return (jnp.cos(angles), jnp.sin(angles))

def rotate(values, cosine_table, sine_table):
    half_width = values.shape[-1] // 2
    lower_half = values[..., :half_width]
    upper_half = values[..., half_width:]
    return jnp.concatenate([lower_half * cosine_table - upper_half * sine_table, upper_half * cosine_table + lower_half * sine_table], axis=-1)

def norm_rows(values, gain_row):
    scale_rows = lax.rsqrt(lax.optimization_barrier(jnp.mean(values * values, axis=-1, keepdims=True)) + EPSILON)
    return low(values * scale_rows * gain_row)

def attend_one(packed):
    query_seq, key_seq, value_seq, doc_seq = packed
    scores = jnp.einsum('qghd,kgd->ghqk', query_seq, key_seq, precision=HIGHEST) * HEAD_DIM ** (-0.5)
    scores = low_back(scores)
    position_line = lax.iota(jnp.int32, doc_seq.shape[0])
    allowed = (position_line[None, :] <= position_line[:, None]) & (doc_seq[:, None] == doc_seq[None, :])
    scores = jnp.where(allowed, scores, NEGATIVE)
    row_peak = lax.optimization_barrier(jnp.max(scores, axis=-1, keepdims=True))
    raised = jnp.exp(scores - row_peak)
    softened = low(raised / lax.optimization_barrier(jnp.sum(raised, axis=-1, keepdims=True)))
    attended = jnp.einsum('ghqk,kgd->qghd', softened, value_seq, precision=HIGHEST)
    return low(low_back(attended))

def layer_apply(residual, doc_ids, cosine_table, sine_table, qkv_w, qkv_b, out_w, gate_w, down_w, gain_rows):
    seq_total, length = doc_ids.shape
    heads_per = HEADS // KV_HEADS
    normed = norm_rows(residual, gain_rows[0])
    projected = low_back(jnp.dot(normed, qkv_w, precision=HIGHEST) + qkv_b)
    projected = projected.reshape(seq_total, length, KV_HEADS, heads_per + 2, HEAD_DIM)
    query_rot = low(rotate(projected[:, :, :, :heads_per], cosine_table[:, :, None, None], sine_table[:, :, None, None]))
    key_rot = low(rotate(projected[:, :, :, heads_per], cosine_table[:, :, None], sine_table[:, :, None]))
    value_low = low(projected[:, :, :, heads_per + 1])
    attended = lax.map(jax.checkpoint(attend_one), (query_rot, key_rot, value_low, doc_ids))
    mixed_rows = attended.reshape(seq_total * length, HEADS * HEAD_DIM)
    after_attn = residual + low_back(jnp.dot(mixed_rows, out_w, precision=HIGHEST))
    normed_two = norm_rows(after_attn, gain_rows[1])
    gate_both = low_back(jnp.dot(normed_two, gate_w.reshape(D, 2 * FF), precision=HIGHEST))
    product = low(jax.nn.silu(gate_both[:, :FF]) * gate_both[:, FF:])
    return after_attn + low_back(jnp.dot(product, down_w, precision=HIGHEST))

def reference(hidden_in, doc_ids, qkv_weight, qkv_bias, out_weight, gate_up, down_weight, norm_gains, cotangent):
    cosine_table, sine_table = rope_tables(doc_ids)
    seq_total, length, width = hidden_in.shape

    def forward_all(residual, qkv_all, bias_all, out_all, gate_all, down_all, gain_all):
        for layer_index in range(LAYERS):
            residual = layer_apply(residual, doc_ids, cosine_table, sine_table, qkv_all[layer_index], bias_all[layer_index], out_all[layer_index], gate_all[layer_index], down_all[layer_index], gain_all[layer_index])
        return residual
    start_rows = hidden_in.astype(jnp.float32).reshape(seq_total * length, width)
    result, pullback = jax.vjp(forward_all, start_rows, qkv_weight.astype(jnp.float32), qkv_bias, out_weight.astype(jnp.float32), gate_up.astype(jnp.float32), down_weight.astype(jnp.float32), norm_gains)
    grads = pullback(cotangent.astype(jnp.float32).reshape(seq_total * length, width))
    hidden_out = result.reshape(seq_total, length, width).astype(jnp.bfloat16)
    input_grad = grads[0].reshape(seq_total, length, width)
    return (hidden_out, input_grad, grads[1], grads[2], grads[3], grads[4], grads[5], grads[6])
```

```python
import functools

import jax
import jax.numpy as jnp
from jax import lax
from jax.experimental import pallas as pl
from jax.experimental.pallas import tpu as pltpu
from jax.sharding import PartitionSpec as P

D = 896
HEADS = 14
KV_HEADS = 2
HEAD_DIM = 64
LAYERS = 2
PER = HEADS // KV_HEADS
QW = PER * HEAD_DIM

EPSILON = 1e-06
ROPE_BASE = 1000000.0
NEGATIVE = -1e30
MESH = pl.DeviceIdType.MESH
LOW = jnp.bfloat16
VMEM = pl.BlockSpec(memory_space=pltpu.VMEM)
LIMIT = 48 * 1024 * 1024


def place():
    return lax.axis_index("wid"), lax.axis_index("grp")


def flip_core(w):
    return w + 1 - 2 * lax.rem(w, 2)


def flip_far(w):
    return lax.rem(w + 2, 4)


def meet(devices):
    barrier = pltpu.get_barrier_semaphore()
    for device in devices:
        pl.semaphore_signal(barrier, inc=1, device_id=device, device_id_type=MESH)
    pl.semaphore_wait(barrier, len(devices))


def partners(kind):
    w, g = place()
    if kind == "grp":
        return g, [({"grp": 1 - g}, 1 - g)]
    ws = [flip_core(w), flip_far(w), flip_far(flip_core(w))]
    if kind == "wid":
        return w, [({"wid": v}, v) for v in ws]
    listed = [({"wid": v, "grp": 1 - g}, v * 2 + 1 - g) for v in [w] + ws]
    listed += [({"wid": v, "grp": g}, v * 2 + g) for v in ws]
    return w * 2 + g, listed


def send(src, dst, ss, rs, device):
    copy = pltpu.make_async_remote_copy(
        src_ref=src, dst_ref=dst, send_sem=ss, recv_sem=rs, device_id=device, device_id_type=MESH
    )
    copy.start()
    return copy


def swap_kernel(kind, gather, x, o, ss, rs):
    me, others = partners(kind)
    meet([d for d, _ in others])
    copies = []
    for j, (device, slot) in enumerate(others):
        src = x if gather else x.at[slot]
        copies.append(send(src, o.at[me], ss.at[j], rs.at[j], device))
    o[me] = x[...] if gather else x[me]
    for copy in copies:
        copy.wait()


def sum_kernel(kind, x, o, buf, ss, rs):
    me, others = partners(kind)
    meet([d for d, _ in others])
    copies = []
    for j, (device, slot) in enumerate(others):
        copies.append(send(x.at[slot], buf.at[j], ss.at[j], rs.at[j], device))
    total = x[me].astype(jnp.float32)
    for j, copy in enumerate(copies):
        copy.wait()
        total = total + buf[j].astype(jnp.float32)
    o[...] = total


def relations():
    w, g = place()
    s = flip_core(w)
    f, fs = flip_far(w), flip_far(s)
    mine = [(w, g), (f, 1 - g), (f, g), (w, 1 - g)]
    theirs = [(s, g), (fs, 1 - g), (fs, g), (s, 1 - g)]
    return mine, theirs


def dev(pair):
    return {"wid": pair[0], "grp": pair[1]}


def slot_of(pair):
    return pair[0] * 2 + pair[1]


def gather_kernel(x, o, ss, rs):
    mine, theirs = relations()
    sibling = dev(theirs[0])
    meet([sibling] + [dev(p) for p in mine[1:]])
    me = slot_of(mine[0])
    copies = [send(x, o.at[me], ss.at[j], rs.at[j], dev(mine[j])) for j in (1, 2, 3)]
    near = send(x, o.at[me], ss.at[0], rs.at[0], sibling)
    o[me] = x[...]
    passed = []
    for j in (2, 3, 1):
        copies[j - 1].wait_recv()
        at = slot_of(mine[j])
        passed.append(send(o.at[at], o.at[at], ss.at[3 + j], rs.at[3 + j], sibling))
    near.wait()
    for j in (1, 2, 3):
        copies[j - 1].wait_send()
    for copy in passed:
        copy.wait()


def scatter_kernel(x, o, first, outgo, second, ss, rs):
    mine, theirs = relations()
    sibling = dev(theirs[0])
    meet([sibling] + [dev(p) for p in mine[1:]])
    order = (1, 2, 3, 0)
    shared = {j: send(x.at[slot_of(theirs[j])], first.at[j], ss.at[j], rs.at[j], sibling) for j in order}
    sent = {}
    for j in (1, 2, 3):
        shared[j].wait_recv()
        pair = x[slot_of(mine[j])].astype(jnp.float32) + first[j].astype(jnp.float32)
        outgo[j - 1] = pair.astype(LOW)
        sent[j] = send(outgo.at[j - 1], second.at[j - 1], ss.at[3 + j], rs.at[3 + j], dev(mine[j]))
    shared[0].wait_recv()
    total = x[slot_of(mine[0])].astype(jnp.float32) + first[0].astype(jnp.float32)
    for j in (2, 3, 1):
        sent[j].wait_recv()
        total = total + second[j - 1].astype(jnp.float32)
    o[...] = total
    for j in order:
        shared[j].wait_send()
    for j in (1, 2, 3):
        sent[j].wait_send()


class Links:
    def __init__(self):
        self.ids = {}

    def call(self, key, kernel, out, scratch, x):
        number = self.ids.setdefault((key, x.shape, str(x.dtype)), len(self.ids))
        return pl.pallas_call(
            kernel,
            out_shape=out,
            in_specs=[VMEM],
            out_specs=VMEM,
            scratch_shapes=scratch,
            compiler_params=pltpu.CompilerParams(
                collective_id=number, has_side_effects=True, vmem_limit_bytes=LIMIT
            ),
        )(x)

    def swap(self, kind, x, gather=False):
        n = {"grp": 2, "wid": 4, "all": 8}[kind]
        shape = (n,) + x.shape if gather else x.shape
        sems = [pltpu.SemaphoreType.DMA((n - 1,))] * 2
        kernel = functools.partial(swap_kernel, kind, gather)
        return self.call(("swap", kind, gather), kernel, jax.ShapeDtypeStruct(shape, x.dtype), sems, x)

    def total(self, kind, x):
        n = x.shape[0]
        scratch = [pltpu.VMEM((n - 1,) + x.shape[1:], x.dtype)]
        scratch += [pltpu.SemaphoreType.DMA((n - 1,))] * 2
        kernel = functools.partial(sum_kernel, kind)
        out = jax.ShapeDtypeStruct(x.shape[1:], jnp.float32)
        return self.call(("sum", kind), kernel, out, scratch, x)

    def gather_all(self, x):
        sems = [pltpu.SemaphoreType.DMA((7,))] * 2
        out = jax.ShapeDtypeStruct((8,) + x.shape, x.dtype)
        return self.call("gather", gather_kernel, out, sems, x).reshape(-1, x.shape[-1])

    def scatter_all(self, x):
        x = x.reshape(8, -1, x.shape[-1])
        tail = x.shape[1:]
        scratch = [pltpu.VMEM((n,) + tail, x.dtype) for n in (4, 3, 3)]
        scratch += [pltpu.SemaphoreType.DMA((7,))] * 2
        out = jax.ShapeDtypeStruct(tail, jnp.float32)
        return self.call("scatter", scatter_kernel, out, scratch, x)


def permute_swap(x):
    n = x.shape[0]
    me = lax.axis_index("wid")
    out = x
    for k in range(1, n):
        other = jnp.bitwise_xor(me, k)
        piece = lax.dynamic_index_in_dim(x, other, 0, keepdims=True)
        piece = lax.ppermute(piece, "wid", [(i, i ^ k) for i in range(n)])
        out = lax.dynamic_update_slice_in_dim(out, piece, other, 0)
    return out


def dot(a, b, over):
    return lax.dot_general(a, b, ((over[0], over[1]), ((), ())), preferred_element_type=jnp.float32)


NN = ((1,), (0,))
NT = ((1,), (1,))
TN = ((0,), (0,))


def soften(q, k, bias):
    scores = dot(q, k, NT) + bias
    raised = jnp.exp(scores - jnp.max(scores, axis=-1, keepdims=True))
    return raised / jnp.sum(raised, axis=-1, keepdims=True)


def attend_kernel(q, kv, bias, o):
    k, v = kv[:, :HEAD_DIM], kv[:, HEAD_DIM:]
    for h in range(PER):
        cols = slice(h * HEAD_DIM, (h + 1) * HEAD_DIM)
        prob = soften(q[:, cols], k, bias[...]).astype(LOW)
        o[:, cols] = dot(prob, v, NN).astype(LOW)


def attend_back_kernel(q, kv, bias, do, dq, dkv):
    k, v = kv[:, :HEAD_DIM], kv[:, HEAD_DIM:]
    dk = jnp.zeros(k.shape, jnp.float32)
    dv = jnp.zeros(k.shape, jnp.float32)
    for h in range(PER):
        cols = slice(h * HEAD_DIM, (h + 1) * HEAD_DIM)
        qh, doh = q[:, cols], do[:, cols]
        soft = soften(qh, k, bias[...])
        dprob = dot(doh, v, NT)
        inner = jnp.sum(soft * dprob, axis=-1, keepdims=True)
        ds = (soft * (dprob - inner)).astype(LOW)
        dq[:, cols] = dot(ds, k, NN) * HEAD_DIM ** (-0.5)
        dk = dk + dot(ds, qh, TN)
        dv = dv + dot(soft.astype(LOW), doh, TN)
    dkv[:, :HEAD_DIM] = dk.astype(LOW)
    dkv[:, HEAD_DIM:] = dv.astype(LOW)


def local_call(kernel, out, args, flops):
    return pl.pallas_call(
        kernel,
        out_shape=out,
        in_specs=[VMEM] * len(args),
        out_specs=jax.tree.map(lambda _: VMEM, out),
        compiler_params=pltpu.CompilerParams(vmem_limit_bytes=LIMIT),
        cost_estimate=pl.CostEstimate(flops=flops, bytes_accessed=4_000_000, transcendentals=2_000_000),
    )(*args)


def rope_tables(doc_ids, offset, span_rows):
    position_grid = lax.broadcasted_iota(jnp.int32, doc_ids.shape, 1)
    change = jnp.concatenate(
        [jnp.ones_like(doc_ids[:, :1]), (doc_ids[:, 1:] != doc_ids[:, :-1]).astype(jnp.int32)],
        axis=1,
    )
    starts = lax.cummax(jnp.where(change > 0, position_grid, 0), axis=1)
    places = (position_grid - starts).astype(jnp.float32)
    places = jnp.transpose(lax.dynamic_slice_in_dim(places, offset, span_rows, 1))
    frequency = ROPE_BASE ** (-jnp.arange(HEAD_DIM // 2, dtype=jnp.float32) / (HEAD_DIM // 2))
    angles = places * frequency[None, :]
    cosine, sine = jnp.cos(angles), jnp.sin(angles)
    still = jnp.ones((span_rows, HEAD_DIM), jnp.float32)
    cosine_all = jnp.concatenate([cosine] * (2 * (PER + 1)) + [still], axis=1)
    sine_all = jnp.concatenate([-sine, sine] * (PER + 1) + [still * 0.0], axis=1)
    return cosine_all, sine_all


def rotate(values, cosine_all, sine_all):
    half = HEAD_DIM // 2
    lane = lax.broadcasted_iota(jnp.int32, values.shape, 1)
    turned = jnp.where(
        lane % HEAD_DIM < half, jnp.roll(values, -half, axis=1), jnp.roll(values, half, axis=1)
    )
    return values * cosine_all + turned * sine_all


def normalize(values, gain_row):
    scale_rows = lax.rsqrt(jnp.sum(values * values, axis=1, keepdims=True) / D + EPSILON)
    return ((values * scale_rows * gain_row).astype(LOW), scale_rows)


def normalize_back(values, gain_row, scale_rows, grad_norm):
    inner_sum = jnp.sum(grad_norm * gain_row * values, axis=1, keepdims=True)
    grad_values = grad_norm * gain_row * scale_rows - values * scale_rows**3 * inner_sum / D
    grad_gain = jnp.sum(grad_norm * values * scale_rows, axis=0)
    return (grad_values, grad_gain)


def per_device(
    hidden_in,
    doc_ids,
    qkv_weight,
    qkv_bias,
    out_weight,
    gate_up,
    down_weight,
    norm_gains,
    cotangent,
):
    _, length, own = hidden_in.shape
    nw, ng, nd = lax.axis_size("wid"), lax.axis_size("grp"), lax.axis_size("dp")
    w, g = place()
    span = length // nw
    rows = span // ng
    ff = down_weight.shape[1]
    part = ff // nw
    offset = w * span
    links = Links()

    weights = []
    gains = lax.all_gather(norm_gains, "wid", axis=2, tiled=True)
    for n in range(LAYERS):
        qkv_w = lax.all_gather(qkv_weight[n], "wid", axis=0, tiled=True)
        out_w = lax.all_gather(out_weight[n], "wid", axis=1, tiled=True)
        both = gate_up[n].reshape(own, 2, nw, part).transpose(2, 1, 0, 3)
        both = permute_swap(both)
        gate_w = both[:, 0].reshape(D, part)
        up_w = both[:, 1].reshape(D, part)
        down_w = permute_swap(down_weight[n].reshape(nw, part, own))
        down_w = down_w.transpose(1, 0, 2).reshape(part, D)
        weights.append((qkv_w, out_w, gate_w, up_w, down_w))

    both = jnp.stack([hidden_in[0], cotangent[0]]).reshape(2, nw, ng, rows, own)
    both = lax.dynamic_index_in_dim(both, g, 2, keepdims=False)
    both = both.transpose(1, 0, 2, 3).reshape(nw, 2 * rows, own)
    both = links.swap("wid", both).transpose(1, 0, 2).reshape(2, rows, D).astype(jnp.float32)
    h, grad = both[0], both[1]

    cosine_all, sine_all = rope_tables(doc_ids, offset, span)
    query_doc = lax.dynamic_slice_in_dim(doc_ids[0], offset, span, 0)
    query_place = offset + lax.iota(jnp.int32, span)
    key_place = lax.iota(jnp.int32, length)
    allowed = (key_place[None, :] <= query_place[:, None]) & (query_doc[:, None] == doc_ids[0][None, :])
    bias = jnp.where(allowed, 0.0, NEGATIVE).astype(jnp.float32)
    scale_row = jnp.concatenate(
        [jnp.full((QW,), HEAD_DIM ** (-0.5), jnp.float32), jnp.ones((2 * HEAD_DIM,), jnp.float32)]
    )
    flops = 4 * PER * span * length * HEAD_DIM

    stored = []
    for n in range(LAYERS):
        qkv_w, out_w, gate_w, up_w, down_w = weights[n]
        a1, r1 = normalize(h, gains[n, 0])
        a1 = links.swap("grp", a1, gather=True).reshape(span, D)
        p = dot(a1, qkv_w, NN) + qkv_bias[n]
        p = (rotate(p, cosine_all, sine_all) * scale_row).astype(LOW)
        q, kv = p[:, :QW], p[:, QW:]
        kv = links.swap("wid", kv, gather=True).reshape(length, 2 * HEAD_DIM)
        o = local_call(
            attend_kernel, jax.ShapeDtypeStruct(q.shape, LOW), (q, kv, bias), flops
        )
        y = dot(o, out_w, NN).astype(LOW).reshape(ng, rows, D)
        h1 = h + links.total("grp", y)
        a2, r2 = normalize(h1, gains[n, 1])
        a2 = links.gather_all(a2)
        gate = dot(a2, gate_w, NN)
        up = dot(a2, up_w, NN)
        m = (jax.nn.silu(gate) * up).astype(LOW)
        gate, up = gate.astype(LOW), up.astype(LOW)
        z = links.scatter_all(dot(m, down_w, NN).astype(LOW))
        stored.append((h, a1, r1, q, kv, o, h1, r2, a2, gate, up, m))
        h = h1 + z

    def to_width(values):
        pieces = values.astype(LOW).reshape(rows, nw, own).transpose(1, 0, 2)
        pieces = jnp.broadcast_to(pieces[:, None], (nw, ng, rows, own)).reshape(nw * ng, rows, own)
        return links.swap("all", pieces).reshape(1, length, own)

    hidden_out = to_width(h)

    grads = []
    small = []
    for n in reversed(range(LAYERS)):
        qkv_w, out_w, gate_w, up_w, down_w = weights[n]
        h, a1, r1, q, kv, o, h1, r2, a2, gate, up, m = stored[n]
        gz = links.gather_all(grad.astype(LOW))
        dm = dot(gz, down_w, NT)
        gate, up = gate.astype(jnp.float32), up.astype(jnp.float32)
        sig = jax.nn.sigmoid(gate)
        dgate = (dm * up * sig * (1.0 + gate * (1.0 - sig))).astype(LOW)
        dup = (dm * (gate * sig)).astype(LOW)
        da2 = links.scatter_all((dot(dgate, gate_w, NT) + dot(dup, up_w, NT)).astype(LOW))
        down_g = dot(m, gz, TN).astype(LOW)
        gate_g = jnp.stack([dot(a2, dgate, TN).astype(LOW), dot(a2, dup, TN).astype(LOW)])
        down_g = permute_swap(down_g.reshape(part, nw, own).transpose(1, 0, 2)).reshape(ff, own)
        down_g = lax.psum_scatter(down_g, "dp", scatter_dimension=0, tiled=True).astype(jnp.float32)
        gate_g = gate_g.reshape(2, nw, nd, own // nd, part).transpose(2, 1, 3, 0, 4)
        gate_g = gate_g.reshape(nd * nw * (own // nd), 2 * part)
        gate_g = lax.psum_scatter(gate_g, "dp", scatter_dimension=0, tiled=True)
        gate_g = permute_swap(gate_g.reshape(nw, own // nd, 2 * part))
        gate_g = gate_g.reshape(nw, own // nd, 2, part).transpose(1, 2, 0, 3)
        gate_g = gate_g.reshape(own // nd, 2, ff).astype(jnp.float32)

        back, gain_two = normalize_back(h1, gains[n, 1], r2, da2)
        g1 = grad + back
        gy = links.swap("grp", g1.astype(LOW), gather=True).reshape(span, D)
        do = dot(gy, out_w, NT).astype(LOW)
        dq, dkv = local_call(
            attend_back_kernel,
            (jax.ShapeDtypeStruct(q.shape, jnp.float32), jax.ShapeDtypeStruct(kv.shape, LOW)),
            (q, kv, bias, do),
            2 * flops,
        )
        dkv = links.total("wid", dkv.reshape(nw, span, 2 * HEAD_DIM))
        dp = rotate(jnp.concatenate([dq, dkv], axis=1), cosine_all, -sine_all).astype(LOW)
        da1 = links.total("grp", dot(dp, qkv_w, NT).astype(LOW).reshape(ng, rows, D))
        back, gain_one = normalize_back(h, gains[n, 0], r1, da1)
        grad = g1 + back

        out_g = dot(o, gy, TN).astype(LOW)
        out_g = out_g.reshape(QW, nw, own).transpose(1, 0, 2).reshape(nw * QW, own)
        out_g = lax.psum_scatter(out_g, ("wid", "dp"), scatter_dimension=0, tiled=True)
        qkv_g = lax.psum_scatter(
            dot(a1, dp, TN).astype(LOW), ("wid", "dp"), scatter_dimension=0, tiled=True
        )
        bias_g = jnp.sum(dp, axis=0, dtype=jnp.float32)
        bias_g = jnp.where(lax.iota(jnp.int32, ng)[:, None] == g, bias_g[None, :], 0.0).reshape(-1)
        small.append(jnp.concatenate([gain_one, gain_two, bias_g]))
        grads.append((qkv_g.astype(jnp.float32), out_g.astype(jnp.float32), gate_g, down_g))

    input_grad = to_width(grad).astype(jnp.float32)
    grads, small = grads[::-1], small[::-1]
    small = lax.psum(jnp.stack(small), ("dp", "grp", "wid"))
    at = lax.axis_index("dp")
    gain_g = small[:, : 2 * D].reshape(LAYERS, 2, D)
    gain_g = lax.dynamic_slice_in_dim(gain_g, w * own + at * (own // nd), own // nd, 2)
    bias_all = small[:, 2 * D :]
    width = bias_all.shape[1] // (ng * nd)
    bias_g = lax.dynamic_slice_in_dim(bias_all, (g * nd + at) * width, width, 1)
    return (
        hidden_out,
        input_grad,
        jnp.stack([member[0] for member in grads]),
        bias_g,
        jnp.stack([member[1] for member in grads]),
        jnp.stack([member[2] for member in grads]),
        jnp.stack([member[3] for member in grads]),
        gain_g,
    )


def solution(mesh):
    placed = (
        P("dp", None, "wid"),
        P("dp", None),
        P(None, "wid", "grp"),
        P(None, "grp"),
        P(None, "grp", "wid"),
        P(None, "wid", None, "grp"),
        P(None, "grp", "wid"),
        P(None, None, "wid"),
        P("dp", None, "wid"),
    )
    return jax.shard_map(
        per_device,
        mesh=mesh,
        in_specs=placed,
        out_specs=(
            P("dp", None, "wid"),
            P("dp", None, "wid"),
            P(None, ("wid", "dp"), "grp"),
            P(None, ("grp", "dp")),
            P(None, ("grp", "dp"), "wid"),
            P(None, ("wid", "dp"), None, "grp"),
            P(None, ("grp", "dp"), "wid"),
            P(None, None, ("wid", "dp")),
        ),
        check_vma=False,
    )
```

```python
import functools

import jax
import jax.numpy as jnp
from jax import lax
from jax.experimental import pallas as pl
from jax.experimental.pallas import tpu as pltpu
from jax.sharding import PartitionSpec as P

D = 896
HEADS = 14
KV_HEADS = 2
HEAD_DIM = 64
LAYERS = 2
PER = HEADS // KV_HEADS
QW = PER * HEAD_DIM

EPSILON = 1e-06
ROPE_BASE = 1000000.0
NEGATIVE = -1e30
MESH = pl.DeviceIdType.MESH
LOW = jnp.bfloat16
VMEM = pl.BlockSpec(memory_space=pltpu.VMEM)
LIMIT = 48 * 1024 * 1024


def place():
    return lax.axis_index("wid"), lax.axis_index("grp")


def flip_core(w):
    return w + 1 - 2 * lax.rem(w, 2)


def flip_far(w):
    return lax.rem(w + 2, 4)


def meet(devices):
    barrier = pltpu.get_barrier_semaphore()
    for device in devices:
        pl.semaphore_signal(barrier, inc=1, device_id=device, device_id_type=MESH)
    pl.semaphore_wait(barrier, len(devices))


def partners(kind):
    w, g = place()
    if kind == "grp":
        return g, [({"grp": 1 - g}, 1 - g)]
    ws = [flip_core(w), flip_far(w), flip_far(flip_core(w))]
    if kind == "wid":
        return w, [({"wid": v}, v) for v in ws]
    listed = [({"wid": v, "grp": 1 - g}, v * 2 + 1 - g) for v in [w] + ws]
    listed += [({"wid": v, "grp": g}, v * 2 + g) for v in ws]
    return w * 2 + g, listed


def send(src, dst, ss, rs, device):
    copy = pltpu.make_async_remote_copy(
        src_ref=src, dst_ref=dst, send_sem=ss, recv_sem=rs, device_id=device, device_id_type=MESH
    )
    copy.start()
    return copy


def swap_kernel(kind, gather, x, o, ss, rs):
    me, others = partners(kind)
    meet([d for d, _ in others])
    copies = []
    for j, (device, slot) in enumerate(others):
        src = x if gather else x.at[slot]
        copies.append(send(src, o.at[me], ss.at[j], rs.at[j], device))
    o[me] = x[...] if gather else x[me]
    for copy in copies:
        copy.wait()


def sum_kernel(kind, x, o, buf, ss, rs):
    me, others = partners(kind)
    meet([d for d, _ in others])
    copies = []
    for j, (device, slot) in enumerate(others):
        copies.append(send(x.at[slot], buf.at[j], ss.at[j], rs.at[j], device))
    total = x[me].astype(jnp.float32)
    for j, copy in enumerate(copies):
        copy.wait()
        total = total + buf[j].astype(jnp.float32)
    o[...] = total


def relations():
    w, g = place()
    s = flip_core(w)
    f, fs = flip_far(w), flip_far(s)
    mine = [(w, g), (f, 1 - g), (f, g), (w, 1 - g)]
    theirs = [(s, g), (fs, 1 - g), (fs, g), (s, 1 - g)]
    return mine, theirs


def dev(pair):
    return {"wid": pair[0], "grp": pair[1]}


def slot_of(pair):
    return pair[0] * 2 + pair[1]


def gather_kernel(x, o, ss, rs):
    mine, theirs = relations()
    sibling = dev(theirs[0])
    meet([sibling] + [dev(p) for p in mine[1:]])
    me = slot_of(mine[0])
    copies = [send(x, o.at[me], ss.at[j], rs.at[j], dev(mine[j])) for j in (1, 2, 3)]
    near = send(x, o.at[me], ss.at[0], rs.at[0], sibling)
    o[me] = x[...]
    passed = []
    for j in (2, 3, 1):
        copies[j - 1].wait_recv()
        at = slot_of(mine[j])
        passed.append(send(o.at[at], o.at[at], ss.at[3 + j], rs.at[3 + j], sibling))
    near.wait()
    for j in (1, 2, 3):
        copies[j - 1].wait_send()
    for copy in passed:
        copy.wait()


def scatter_kernel(x, o, first, outgo, second, ss, rs):
    mine, theirs = relations()
    sibling = dev(theirs[0])
    meet([sibling] + [dev(p) for p in mine[1:]])
    order = (1, 2, 3, 0)
    shared = {j: send(x.at[slot_of(theirs[j])], first.at[j], ss.at[j], rs.at[j], sibling) for j in order}
    sent = {}
    for j in (1, 2, 3):
        shared[j].wait_recv()
        pair = x[slot_of(mine[j])].astype(jnp.float32) + first[j].astype(jnp.float32)
        outgo[j - 1] = pair.astype(LOW)
        sent[j] = send(outgo.at[j - 1], second.at[j - 1], ss.at[3 + j], rs.at[3 + j], dev(mine[j]))
    shared[0].wait_recv()
    total = x[slot_of(mine[0])].astype(jnp.float32) + first[0].astype(jnp.float32)
    for j in (2, 3, 1):
        sent[j].wait_recv()
        total = total + second[j - 1].astype(jnp.float32)
    o[...] = total
    for j in order:
        shared[j].wait_send()
    for j in (1, 2, 3):
        sent[j].wait_send()


def gather_wid_kernel(*refs):
    count = (len(refs) - 2) // 2
    xs, outs, (ss, rs) = refs[:count], refs[count : 2 * count], refs[2 * count :]
    w, _ = place()
    sibling, far = flip_core(w), flip_far(w)
    meet([{"wid": sibling}, {"wid": far}])
    far_copies = [
        send(x, o.at[w], ss.at[i, 0], rs.at[i, 0], {"wid": far}) for i, (x, o) in enumerate(zip(xs, outs))
    ]
    copies = [
        send(x, o.at[w], ss.at[i, 1], rs.at[i, 1], {"wid": sibling})
        for i, (x, o) in enumerate(zip(xs, outs))
    ]
    for x, o in zip(xs, outs):
        o[w] = x[...]
    for i, o in enumerate(outs):
        far_copies[i].wait_recv()
        copies.append(send(o.at[far], o.at[far], ss.at[i, 2], rs.at[i, 2], {"wid": sibling}))
    for copy in copies:
        copy.wait()
    for copy in far_copies:
        copy.wait_send()


def gather_dp_kernel(n, x, o, ss, rs):
    me = lax.axis_index("dp")
    others = [lax.rem(me + j, n) for j in range(1, n)]
    meet([{"dp": v} for v in others])
    copies = [
        send(x, o.at[me], ss.at[j], rs.at[j], {"dp": v}) for j, v in enumerate(others)
    ]
    o[me] = x[...]
    for copy in copies:
        copy.wait()


def expected(us):
    return pl.CostEstimate(
        flops=int(us * 1e9), bytes_accessed=int(us * 3e6), transcendentals=0
    )


class Links:
    def __init__(self):
        self.ids = {}

    def call(self, key, kernel, out, scratch, *xs, us=8):
        shapes = tuple((x.shape, str(x.dtype)) for x in xs)
        number = self.ids.setdefault((key, shapes), len(self.ids))
        return pl.pallas_call(
            kernel,
            out_shape=out,
            in_specs=[VMEM] * len(xs),
            out_specs=jax.tree.map(lambda _: VMEM, out),
            cost_estimate=expected(us),
            scratch_shapes=scratch,
            compiler_params=pltpu.CompilerParams(
                collective_id=number, has_side_effects=True, vmem_limit_bytes=LIMIT
            ),
        )(*xs)

    def swap(self, kind, x, gather=False):
        n = {"grp": 2, "wid": 4, "all": 8}[kind]
        shape = (n,) + x.shape if gather else x.shape
        sems = [pltpu.SemaphoreType.DMA((n - 1,))] * 2
        kernel = functools.partial(swap_kernel, kind, gather)
        return self.call(("swap", kind, gather), kernel, jax.ShapeDtypeStruct(shape, x.dtype), sems, x)

    def total(self, kind, x):
        n = x.shape[0]
        scratch = [pltpu.VMEM((n - 1,) + x.shape[1:], x.dtype)]
        scratch += [pltpu.SemaphoreType.DMA((n - 1,))] * 2
        kernel = functools.partial(sum_kernel, kind)
        out = jax.ShapeDtypeStruct(x.shape[1:], jnp.float32)
        return self.call(("sum", kind), kernel, out, scratch, x)

    def gather_wid(self, *xs):
        sems = [pltpu.SemaphoreType.DMA((len(xs), 3))] * 2
        out = [jax.ShapeDtypeStruct((4,) + x.shape, x.dtype) for x in xs]
        return self.call("widen", gather_wid_kernel, out, sems, *xs, us=12)

    def gather_dp(self, x):
        n = lax.axis_size("dp")
        sems = [pltpu.SemaphoreType.DMA((n - 1,))] * 2
        out = jax.ShapeDtypeStruct((n,) + x.shape, x.dtype)
        return self.call("dp", functools.partial(gather_dp_kernel, n), out, sems, x)

    def gather_all(self, x):
        sems = [pltpu.SemaphoreType.DMA((7,))] * 2
        out = jax.ShapeDtypeStruct((8,) + x.shape, x.dtype)
        return self.call("gather", gather_kernel, out, sems, x, us=15).reshape(-1, x.shape[-1])

    def scatter_all(self, x):
        x = x.reshape(8, -1, x.shape[-1])
        tail = x.shape[1:]
        scratch = [pltpu.VMEM((n,) + tail, x.dtype) for n in (4, 3, 3)]
        scratch += [pltpu.SemaphoreType.DMA((7,))] * 2
        out = jax.ShapeDtypeStruct(tail, jnp.float32)
        return self.call("scatter", scatter_kernel, out, scratch, x, us=15)


def permute_swap(x):
    n = x.shape[0]
    me = lax.axis_index("wid")
    out = x
    for k in range(1, n):
        other = jnp.bitwise_xor(me, k)
        piece = lax.dynamic_index_in_dim(x, other, 0, keepdims=True)
        piece = lax.ppermute(piece, "wid", [(i, i ^ k) for i in range(n)])
        out = lax.dynamic_update_slice_in_dim(out, piece, other, 0)
    return out


def dot(a, b, over):
    return lax.dot_general(a, b, ((over[0], over[1]), ((), ())), preferred_element_type=jnp.float32)


NN = ((1,), (0,))
NT = ((1,), (1,))
TN = ((0,), (0,))


def soften(q, k, bias):
    scores = dot(q, k, NT) + bias
    raised = jnp.exp(scores - jnp.max(scores, axis=-1, keepdims=True))
    return raised / jnp.sum(raised, axis=-1, keepdims=True)


def attend_kernel(q, kv, bias, o):
    k, v = kv[:, :HEAD_DIM], kv[:, HEAD_DIM:]
    for h in range(PER):
        cols = slice(h * HEAD_DIM, (h + 1) * HEAD_DIM)
        prob = soften(q[:, cols], k, bias[...]).astype(LOW)
        o[:, cols] = dot(prob, v, NN).astype(LOW)


def attend_back_kernel(q, kv, bias, do, dq, dkv):
    k, v = kv[:, :HEAD_DIM], kv[:, HEAD_DIM:]
    dk = jnp.zeros(k.shape, jnp.float32)
    dv = jnp.zeros(k.shape, jnp.float32)
    for h in range(PER):
        cols = slice(h * HEAD_DIM, (h + 1) * HEAD_DIM)
        qh, doh = q[:, cols], do[:, cols]
        soft = soften(qh, k, bias[...])
        dprob = dot(doh, v, NT)
        inner = jnp.sum(soft * dprob, axis=-1, keepdims=True)
        ds = (soft * (dprob - inner)).astype(LOW)
        dq[:, cols] = dot(ds, k, NN) * HEAD_DIM ** (-0.5)
        dk = dk + dot(ds, qh, TN)
        dv = dv + dot(soft.astype(LOW), doh, TN)
    dkv[:, :HEAD_DIM] = dk.astype(LOW)
    dkv[:, HEAD_DIM:] = dv.astype(LOW)


def local_call(kernel, out, args, us):
    return pl.pallas_call(
        kernel,
        out_shape=out,
        in_specs=[VMEM] * len(args),
        out_specs=jax.tree.map(lambda _: VMEM, out),
        compiler_params=pltpu.CompilerParams(vmem_limit_bytes=LIMIT),
        cost_estimate=expected(us),
    )(*args)


def rope_tables(doc_ids, offset, span_rows):
    position_grid = lax.broadcasted_iota(jnp.int32, doc_ids.shape, 1)
    change = jnp.concatenate(
        [jnp.ones_like(doc_ids[:, :1]), (doc_ids[:, 1:] != doc_ids[:, :-1]).astype(jnp.int32)],
        axis=1,
    )
    starts = lax.cummax(jnp.where(change > 0, position_grid, 0), axis=1)
    places = (position_grid - starts).astype(jnp.float32)
    places = jnp.transpose(lax.dynamic_slice_in_dim(places, offset, span_rows, 1))
    frequency = ROPE_BASE ** (-jnp.arange(HEAD_DIM // 2, dtype=jnp.float32) / (HEAD_DIM // 2))
    angles = places * frequency[None, :]
    cosine, sine = jnp.cos(angles), jnp.sin(angles)
    still = jnp.ones((span_rows, HEAD_DIM), jnp.float32)
    cosine_all = jnp.concatenate([cosine] * (2 * (PER + 1)) + [still], axis=1)
    sine_all = jnp.concatenate([-sine, sine] * (PER + 1) + [still * 0.0], axis=1)
    return cosine_all, sine_all


def rotate(values, cosine_all, sine_all):
    half = HEAD_DIM // 2
    lane = lax.broadcasted_iota(jnp.int32, values.shape, 1)
    turned = jnp.where(
        lane % HEAD_DIM < half, jnp.roll(values, -half, axis=1), jnp.roll(values, half, axis=1)
    )
    return values * cosine_all + turned * sine_all


def normalize(values, gain_row):
    scale_rows = lax.rsqrt(jnp.sum(values * values, axis=1, keepdims=True) / D + EPSILON)
    return ((values * scale_rows * gain_row).astype(LOW), scale_rows)


def normalize_back(values, gain_row, scale_rows, grad_norm):
    inner_sum = jnp.sum(grad_norm * gain_row * values, axis=1, keepdims=True)
    grad_values = grad_norm * gain_row * scale_rows - values * scale_rows**3 * inner_sum / D
    grad_gain = jnp.sum(grad_norm * values * scale_rows, axis=0)
    return (grad_values, grad_gain)


def per_device(
    hidden_in,
    doc_ids,
    qkv_weight,
    qkv_bias,
    out_weight,
    gate_up,
    down_weight,
    norm_gains,
    cotangent,
):
    _, length, own = hidden_in.shape
    nw, ng, nd = lax.axis_size("wid"), lax.axis_size("grp"), lax.axis_size("dp")
    w, g = place()
    span = length // nw
    rows = span // ng
    ff = down_weight.shape[1]
    part = -(-ff // (nw * 128)) * 128
    pad = nw * part - ff
    offset = w * span
    links = Links()

    weights = []
    (gains,) = links.gather_wid(norm_gains.reshape(2 * LAYERS, own))
    gains = gains.transpose(1, 0, 2).reshape(LAYERS, 2, D)
    for n in range(LAYERS):
        qkv_w, out_w = links.gather_wid(qkv_weight[n], out_weight[n])
        qkv_w = qkv_w.reshape(D, -1)
        out_w = out_w.transpose(1, 0, 2).reshape(QW, D)
        both = jnp.pad(gate_up[n], ((0, 0), (0, 0), (0, pad)))
        both = both.reshape(own, 2, nw, part).transpose(2, 1, 0, 3)
        both = permute_swap(both)
        gate_w = both[:, 0].reshape(D, part)
        up_w = both[:, 1].reshape(D, part)
        down_w = permute_swap(jnp.pad(down_weight[n], ((0, pad), (0, 0))).reshape(nw, part, own))
        down_w = down_w.transpose(1, 0, 2).reshape(part, D)
        weights.append((qkv_w, out_w, gate_w, up_w, down_w))

    both = jnp.stack([hidden_in[0], cotangent[0]]).reshape(2, nw, ng, rows, own)
    both = lax.dynamic_index_in_dim(both, g, 2, keepdims=False)
    both = both.transpose(1, 0, 2, 3).reshape(nw, 2 * rows, own)
    both = links.swap("wid", both).transpose(1, 0, 2).reshape(2, rows, D).astype(jnp.float32)
    h, grad = both[0], both[1]

    cosine_all, sine_all = rope_tables(doc_ids, offset, span)
    query_doc = lax.dynamic_slice_in_dim(doc_ids[0], offset, span, 0)
    query_place = offset + lax.iota(jnp.int32, span)
    key_place = lax.iota(jnp.int32, length)
    allowed = (key_place[None, :] <= query_place[:, None]) & (query_doc[:, None] == doc_ids[0][None, :])
    bias = jnp.where(allowed, 0.0, NEGATIVE).astype(jnp.float32)
    scale_row = jnp.concatenate(
        [jnp.full((QW,), HEAD_DIM ** (-0.5), jnp.float32), jnp.ones((2 * HEAD_DIM,), jnp.float32)]
    )

    stored = []
    for n in range(LAYERS):
        qkv_w, out_w, gate_w, up_w, down_w = weights[n]
        a1, r1 = normalize(h, gains[n, 0])
        a1 = links.swap("grp", a1, gather=True).reshape(span, D)
        p = dot(a1, qkv_w, NN) + qkv_bias[n]
        p = (rotate(p, cosine_all, sine_all) * scale_row).astype(LOW)
        q, kv = p[:, :QW], p[:, QW:]
        kv = links.swap("wid", kv, gather=True).reshape(length, 2 * HEAD_DIM)
        o = local_call(
            attend_kernel, jax.ShapeDtypeStruct(q.shape, LOW), (q, kv, bias), 4
        )
        y = dot(o, out_w, NN).astype(LOW).reshape(ng, rows, D)
        h1 = h + links.total("grp", y)
        a2, r2 = normalize(h1, gains[n, 1])
        a2 = links.gather_all(a2)
        gate = dot(a2, gate_w, NN)
        up = dot(a2, up_w, NN)
        m = (jax.nn.silu(gate) * up).astype(LOW)
        gate, up = gate.astype(LOW), up.astype(LOW)
        z = links.scatter_all(dot(m, down_w, NN).astype(LOW))
        stored.append((h, a1, r1, q, kv, o, h1, r2, a2, gate, up, m))
        h = h1 + z

    def to_width(values):
        pieces = values.astype(LOW).reshape(rows, nw, own).transpose(1, 0, 2)
        pieces = jnp.broadcast_to(pieces[:, None], (nw, ng, rows, own)).reshape(nw * ng, rows, own)
        return links.swap("all", pieces).reshape(1, length, own)

    hidden_out = to_width(h)

    grads = []
    small = []
    pending = ()
    for n in reversed(range(LAYERS)):
        qkv_w, out_w, gate_w, up_w, down_w = weights[n]
        h, a1, r1, q, kv, o, h1, r2, a2, gate, up, m = stored[n]
        gz = links.gather_all(grad.astype(LOW))
        dm = dot(gz, down_w, NT)
        gate, up = gate.astype(jnp.float32), up.astype(jnp.float32)
        sig = jax.nn.sigmoid(gate)
        dgate = (dm * up * sig * (1.0 + gate * (1.0 - sig))).astype(LOW)
        dup = (dm * (gate * sig)).astype(LOW)
        da2 = (dot(dgate, gate_w, NT) + dot(dup, up_w, NT)).astype(LOW)
        down_g = dot(m, gz, TN).astype(LOW)
        gate_g = jnp.stack([dot(a2, dgate, TN).astype(LOW), dot(a2, dup, TN).astype(LOW)])
        da2, down_g, gate_g, pending = lax.optimization_barrier((da2, down_g, gate_g, pending))
        if pending:
            grads.append(pending)
        da2 = links.scatter_all(da2)
        down_g = permute_swap(down_g.reshape(part, nw, own).transpose(1, 0, 2))
        down_g = down_g.reshape(nw * part, own)[:ff]
        down_g = lax.psum_scatter(down_g, "dp", scatter_dimension=0, tiled=True)
        gate_g = gate_g.reshape(2, nw, nd, own // nd, part).transpose(2, 1, 3, 0, 4)
        gate_g = gate_g.reshape(nd * nw * (own // nd), 2 * part)
        gate_g = lax.psum_scatter(gate_g, "dp", scatter_dimension=0, tiled=True)
        gate_g = permute_swap(gate_g.reshape(nw, own // nd, 2 * part))
        gate_g = gate_g.reshape(nw, own // nd, 2, part).transpose(1, 2, 0, 3)
        gate_g = gate_g.reshape(own // nd, 2, nw * part)[:, :, :ff]

        back, gain_two = normalize_back(h1, gains[n, 1], r2, da2)
        g1 = grad + back
        gy = links.swap("grp", g1.astype(LOW), gather=True).reshape(span, D)
        do = dot(gy, out_w, NT).astype(LOW)
        dq, dkv = local_call(
            attend_back_kernel,
            (jax.ShapeDtypeStruct(q.shape, jnp.float32), jax.ShapeDtypeStruct(kv.shape, LOW)),
            (q, kv, bias, do),
            8,
        )
        dkv = links.total("wid", dkv.reshape(nw, span, 2 * HEAD_DIM))
        dp = rotate(jnp.concatenate([dq, dkv], axis=1), cosine_all, -sine_all).astype(LOW)
        da1 = links.total("grp", dot(dp, qkv_w, NT).astype(LOW).reshape(ng, rows, D))
        back, gain_one = normalize_back(h, gains[n, 0], r1, da1)
        grad = g1 + back

        out_g = dot(o, gy, TN).astype(LOW)
        out_g = out_g.reshape(QW, nw, own).transpose(1, 0, 2).reshape(nw * QW, own)
        out_g = lax.psum_scatter(out_g, ("wid", "dp"), scatter_dimension=0, tiled=True)
        qkv_g = lax.psum_scatter(
            dot(a1, dp, TN).astype(LOW), ("wid", "dp"), scatter_dimension=0, tiled=True
        )
        bias_g = jnp.sum(dp, axis=0, dtype=jnp.float32)
        bias_g = jnp.where(lax.iota(jnp.int32, ng)[:, None] == g, bias_g[None, :], 0.0).reshape(-1)
        small.append(jnp.concatenate([gain_one, gain_two, bias_g]))
        pending = (qkv_g, out_g, gate_g, down_g)

    grad, down_g, gate_g = lax.optimization_barrier((grad, pending[3], pending[2]))
    grads.append(pending[:2] + (gate_g, down_g))
    grads = [tuple(part_g.astype(jnp.float32) for part_g in member) for member in grads]
    input_grad = to_width(grad).astype(jnp.float32)
    grads, small = grads[::-1], small[::-1]
    small = jnp.stack(small)
    flat = small.reshape(-1, 128)
    flat = jnp.sum(links.swap("all", flat, gather=True), axis=0)
    small = jnp.sum(links.gather_dp(flat), axis=0).reshape(small.shape)
    at = lax.axis_index("dp")
    gain_g = small[:, : 2 * D].reshape(LAYERS, 2, D)
    gain_g = lax.dynamic_slice_in_dim(gain_g, w * own + at * (own // nd), own // nd, 2)
    bias_all = small[:, 2 * D :]
    width = bias_all.shape[1] // (ng * nd)
    bias_g = lax.dynamic_slice_in_dim(bias_all, (g * nd + at) * width, width, 1)
    return (
        hidden_out,
        input_grad,
        jnp.stack([member[0] for member in grads]),
        bias_g,
        jnp.stack([member[1] for member in grads]),
        jnp.stack([member[2] for member in grads]),
        jnp.stack([member[3] for member in grads]),
        gain_g,
    )


def solution(mesh):
    placed = (
        P("dp", None, "wid"),
        P("dp", None),
        P(None, "wid", "grp"),
        P(None, "grp"),
        P(None, "grp", "wid"),
        P(None, "wid", None, "grp"),
        P(None, "grp", "wid"),
        P(None, None, "wid"),
        P("dp", None, "wid"),
    )
    return jax.shard_map(
        per_device,
        mesh=mesh,
        in_specs=placed,
        out_specs=(
            P("dp", None, "wid"),
            P("dp", None, "wid"),
            P(None, ("wid", "dp"), "grp"),
            P(None, ("grp", "dp")),
            P(None, ("grp", "dp"), "wid"),
            P(None, ("wid", "dp"), None, "grp"),
            P(None, ("grp", "dp"), "wid"),
            P(None, None, ("wid", "dp")),
        ),
        check_vma=False,
    )
```

```python
import functools

import jax
import jax.numpy as jnp
from jax import lax
from jax.experimental import pallas as pl
from jax.experimental.pallas import tpu as pltpu
from jax.sharding import PartitionSpec as P

D = 896
HEADS = 14
KV_HEADS = 2
HEAD_DIM = 64
LAYERS = 2
PER = HEADS // KV_HEADS
QW = PER * HEAD_DIM

EPSILON = 1e-06
ROPE_BASE = 1000000.0
NEGATIVE = -1e30
MESH = pl.DeviceIdType.MESH
LOW = jnp.bfloat16
VMEM = pl.BlockSpec(memory_space=pltpu.VMEM)
LIMIT = 48 * 1024 * 1024


def place():
    return lax.axis_index("wid"), lax.axis_index("grp")


def flip_core(w):
    return w + 1 - 2 * lax.rem(w, 2)


def flip_far(w):
    return lax.rem(w + 2, 4)


def meet(devices):
    barrier = pltpu.get_barrier_semaphore()
    for device in devices:
        pl.semaphore_signal(barrier, inc=1, device_id=device, device_id_type=MESH)
    pl.semaphore_wait(barrier, len(devices))


def partners(kind):
    w, g = place()
    if kind == "grp":
        return g, [({"grp": 1 - g}, 1 - g)]
    ws = [flip_core(w), flip_far(w), flip_far(flip_core(w))]
    if kind == "wid":
        return w, [({"wid": v}, v) for v in ws]
    listed = [({"wid": v, "grp": 1 - g}, v * 2 + 1 - g) for v in [w] + ws]
    listed += [({"wid": v, "grp": g}, v * 2 + g) for v in ws]
    return w * 2 + g, listed


def send(src, dst, ss, rs, device):
    copy = pltpu.make_async_remote_copy(
        src_ref=src, dst_ref=dst, send_sem=ss, recv_sem=rs, device_id=device, device_id_type=MESH
    )
    copy.start()
    return copy


def swap_kernel(kind, gather, x, o, ss, rs):
    me, others = partners(kind)
    meet([d for d, _ in others])
    copies = []
    for j, (device, slot) in enumerate(others):
        src = x if gather else x.at[slot]
        copies.append(send(src, o.at[me], ss.at[j], rs.at[j], device))
    o[me] = x[...] if gather else x[me]
    for copy in copies:
        copy.wait()


def sum_kernel(kind, x, o, buf, ss, rs):
    me, others = partners(kind)
    meet([d for d, _ in others])
    copies = []
    for j, (device, slot) in enumerate(others):
        copies.append(send(x.at[slot], buf.at[j], ss.at[j], rs.at[j], device))
    total = x[me].astype(jnp.float32)
    for j, copy in enumerate(copies):
        copy.wait()
        total = total + buf[j].astype(jnp.float32)
    o[...] = total


def relations():
    w, g = place()
    s = flip_core(w)
    f, fs = flip_far(w), flip_far(s)
    mine = [(w, g), (f, 1 - g), (f, g), (w, 1 - g)]
    theirs = [(s, g), (fs, 1 - g), (fs, g), (s, 1 - g)]
    return mine, theirs


def dev(pair):
    return {"wid": pair[0], "grp": pair[1]}


def slot_of(pair):
    return pair[0] * 2 + pair[1]


def gather_kernel(x, o, ss, rs):
    mine, theirs = relations()
    sibling = dev(theirs[0])
    meet([sibling] + [dev(p) for p in mine[1:]])
    me = slot_of(mine[0])
    copies = [send(x, o.at[me], ss.at[j], rs.at[j], dev(mine[j])) for j in (1, 2, 3)]
    near = send(x, o.at[me], ss.at[0], rs.at[0], sibling)
    o[me] = x[...]
    passed = []
    for j in (2, 3, 1):
        copies[j - 1].wait_recv()
        at = slot_of(mine[j])
        passed.append(send(o.at[at], o.at[at], ss.at[3 + j], rs.at[3 + j], sibling))
    near.wait()
    for j in (1, 2, 3):
        copies[j - 1].wait_send()
    for copy in passed:
        copy.wait()


def scatter_kernel(x, o, first, outgo, second, ss, rs):
    mine, theirs = relations()
    sibling = dev(theirs[0])
    meet([sibling] + [dev(p) for p in mine[1:]])
    order = (1, 2, 3, 0)
    shared = {j: send(x.at[slot_of(theirs[j])], first.at[j], ss.at[j], rs.at[j], sibling) for j in order}
    sent = {}
    for j in (1, 2, 3):
        shared[j].wait_recv()
        pair = x[slot_of(mine[j])].astype(jnp.float32) + first[j].astype(jnp.float32)
        outgo[j - 1] = pair.astype(LOW)
        sent[j] = send(outgo.at[j - 1], second.at[j - 1], ss.at[3 + j], rs.at[3 + j], dev(mine[j]))
    shared[0].wait_recv()
    total = x[slot_of(mine[0])].astype(jnp.float32) + first[0].astype(jnp.float32)
    for j in (2, 3, 1):
        sent[j].wait_recv()
        total = total + second[j - 1].astype(jnp.float32)
    o[...] = total
    for j in order:
        shared[j].wait_send()
    for j in (1, 2, 3):
        sent[j].wait_send()


def gather_wid_kernel(*refs):
    count = (len(refs) - 2) // 2
    xs, outs, (ss, rs) = refs[:count], refs[count : 2 * count], refs[2 * count :]
    w, _ = place()
    sibling, far = flip_core(w), flip_far(w)
    meet([{"wid": sibling}, {"wid": far}])
    far_copies = [
        send(x, o.at[w], ss.at[i, 0], rs.at[i, 0], {"wid": far}) for i, (x, o) in enumerate(zip(xs, outs))
    ]
    copies = [
        send(x, o.at[w], ss.at[i, 1], rs.at[i, 1], {"wid": sibling})
        for i, (x, o) in enumerate(zip(xs, outs))
    ]
    for x, o in zip(xs, outs):
        o[w] = x[...]
    for i, o in enumerate(outs):
        far_copies[i].wait_recv()
        copies.append(send(o.at[far], o.at[far], ss.at[i, 2], rs.at[i, 2], {"wid": sibling}))
    for copy in copies:
        copy.wait()
    for copy in far_copies:
        copy.wait_send()


def gather_dp_kernel(n, x, o, ss, rs):
    me = lax.axis_index("dp")
    others = [lax.rem(me + j, n) for j in range(1, n)]
    meet([{"dp": v} for v in others])
    copies = [
        send(x, o.at[me], ss.at[j], rs.at[j], {"dp": v}) for j, v in enumerate(others)
    ]
    o[me] = x[...]
    for copy in copies:
        copy.wait()


def expected(us):
    return pl.CostEstimate(
        flops=int(us * 1e9), bytes_accessed=int(us * 3e6), transcendentals=0
    )


class Links:
    def __init__(self):
        self.ids = {}

    def call(self, key, kernel, out, scratch, *xs, us=8):
        shapes = tuple((x.shape, str(x.dtype)) for x in xs)
        number = self.ids.setdefault((key, shapes), len(self.ids))
        return pl.pallas_call(
            kernel,
            out_shape=out,
            in_specs=[VMEM] * len(xs),
            out_specs=jax.tree.map(lambda _: VMEM, out),
            cost_estimate=expected(us),
            scratch_shapes=scratch,
            compiler_params=pltpu.CompilerParams(
                collective_id=number, has_side_effects=True, vmem_limit_bytes=LIMIT
            ),
        )(*xs)

    def swap(self, kind, x, gather=False):
        n = {"grp": 2, "wid": 4, "all": 8}[kind]
        shape = (n,) + x.shape if gather else x.shape
        sems = [pltpu.SemaphoreType.DMA((n - 1,))] * 2
        kernel = functools.partial(swap_kernel, kind, gather)
        return self.call(("swap", kind, gather), kernel, jax.ShapeDtypeStruct(shape, x.dtype), sems, x)

    def total(self, kind, x):
        n = x.shape[0]
        scratch = [pltpu.VMEM((n - 1,) + x.shape[1:], x.dtype)]
        scratch += [pltpu.SemaphoreType.DMA((n - 1,))] * 2
        kernel = functools.partial(sum_kernel, kind)
        out = jax.ShapeDtypeStruct(x.shape[1:], jnp.float32)
        return self.call(("sum", kind), kernel, out, scratch, x)

    def gather_wid(self, *xs):
        sems = [pltpu.SemaphoreType.DMA((len(xs), 3))] * 2
        out = [jax.ShapeDtypeStruct((4,) + x.shape, x.dtype) for x in xs]
        return self.call("widen", gather_wid_kernel, out, sems, *xs, us=12)

    def gather_dp(self, x):
        n = lax.axis_size("dp")
        sems = [pltpu.SemaphoreType.DMA((n - 1,))] * 2
        out = jax.ShapeDtypeStruct((n,) + x.shape, x.dtype)
        return self.call("dp", functools.partial(gather_dp_kernel, n), out, sems, x)

    def gather_all(self, x):
        sems = [pltpu.SemaphoreType.DMA((7,))] * 2
        out = jax.ShapeDtypeStruct((8,) + x.shape, x.dtype)
        return self.call("gather", gather_kernel, out, sems, x, us=15).reshape(-1, x.shape[-1])

    def scatter_all(self, x):
        x = x.reshape(8, -1, x.shape[-1])
        tail = x.shape[1:]
        scratch = [pltpu.VMEM((n,) + tail, x.dtype) for n in (4, 3, 3)]
        scratch += [pltpu.SemaphoreType.DMA((7,))] * 2
        out = jax.ShapeDtypeStruct(tail, jnp.float32)
        return self.call("scatter", scatter_kernel, out, scratch, x, us=15)


def dot(a, b, over):
    return lax.dot_general(a, b, ((over[0], over[1]), ((), ())), preferred_element_type=jnp.float32)


NN = ((1,), (0,))
NT = ((1,), (1,))
TN = ((0,), (0,))


def soften(q, k, bias):
    scores = dot(q, k, NT) + bias
    raised = jnp.exp(scores - jnp.max(scores, axis=-1, keepdims=True))
    return raised / jnp.sum(raised, axis=-1, keepdims=True)


def attend_kernel(q, kv, bias, o):
    k, v = kv[:, :HEAD_DIM], kv[:, HEAD_DIM:]
    for h in range(PER):
        cols = slice(h * HEAD_DIM, (h + 1) * HEAD_DIM)
        prob = soften(q[:, cols], k, bias[...]).astype(LOW)
        o[:, cols] = dot(prob, v, NN).astype(LOW)


def attend_back_kernel(q, kv, bias, do, dq, dkv):
    k, v = kv[:, :HEAD_DIM], kv[:, HEAD_DIM:]
    dk = jnp.zeros(k.shape, jnp.float32)
    dv = jnp.zeros(k.shape, jnp.float32)
    for h in range(PER):
        cols = slice(h * HEAD_DIM, (h + 1) * HEAD_DIM)
        qh, doh = q[:, cols], do[:, cols]
        soft = soften(qh, k, bias[...])
        dprob = dot(doh, v, NT)
        inner = jnp.sum(soft * dprob, axis=-1, keepdims=True)
        ds = (soft * (dprob - inner)).astype(LOW)
        dq[:, cols] = dot(ds, k, NN) * HEAD_DIM ** (-0.5)
        dk = dk + dot(ds, qh, TN)
        dv = dv + dot(soft.astype(LOW), doh, TN)
    dkv[:, :HEAD_DIM] = dk.astype(LOW)
    dkv[:, HEAD_DIM:] = dv.astype(LOW)


def local_call(kernel, out, args, us):
    return pl.pallas_call(
        kernel,
        out_shape=out,
        in_specs=[VMEM] * len(args),
        out_specs=jax.tree.map(lambda _: VMEM, out),
        compiler_params=pltpu.CompilerParams(vmem_limit_bytes=LIMIT),
        cost_estimate=expected(us),
    )(*args)


def rope_tables(doc_ids, offset, span_rows):
    position_grid = lax.broadcasted_iota(jnp.int32, doc_ids.shape, 1)
    change = jnp.concatenate(
        [jnp.ones_like(doc_ids[:, :1]), (doc_ids[:, 1:] != doc_ids[:, :-1]).astype(jnp.int32)],
        axis=1,
    )
    starts = lax.cummax(jnp.where(change > 0, position_grid, 0), axis=1)
    places = (position_grid - starts).astype(jnp.float32)
    places = jnp.transpose(lax.dynamic_slice_in_dim(places, offset, span_rows, 1))
    frequency = ROPE_BASE ** (-jnp.arange(HEAD_DIM // 2, dtype=jnp.float32) / (HEAD_DIM // 2))
    angles = places * frequency[None, :]
    cosine, sine = jnp.cos(angles), jnp.sin(angles)
    still = jnp.ones((span_rows, HEAD_DIM), jnp.float32)
    cosine_all = jnp.concatenate([cosine] * (2 * (PER + 1)) + [still], axis=1)
    sine_all = jnp.concatenate([-sine, sine] * (PER + 1) + [still * 0.0], axis=1)
    return cosine_all, sine_all


def rotate(values, cosine_all, sine_all):
    half = HEAD_DIM // 2
    lane = lax.broadcasted_iota(jnp.int32, values.shape, 1)
    turned = jnp.where(
        lane % HEAD_DIM < half, jnp.roll(values, -half, axis=1), jnp.roll(values, half, axis=1)
    )
    return values * cosine_all + turned * sine_all


def normalize(values, gain_row):
    scale_rows = lax.rsqrt(jnp.sum(values * values, axis=1, keepdims=True) / D + EPSILON)
    return ((values * scale_rows * gain_row).astype(LOW), scale_rows)


def normalize_back(values, gain_row, scale_rows, grad_norm):
    inner_sum = jnp.sum(grad_norm * gain_row * values, axis=1, keepdims=True)
    grad_values = grad_norm * gain_row * scale_rows - values * scale_rows**3 * inner_sum / D
    grad_gain = jnp.sum(grad_norm * values * scale_rows, axis=0)
    return (grad_values, grad_gain)


def per_device(
    hidden_in,
    doc_ids,
    qkv_weight,
    qkv_bias,
    out_weight,
    gate_up,
    down_weight,
    norm_gains,
    cotangent,
):
    _, length, own = hidden_in.shape
    nw, ng, nd = lax.axis_size("wid"), lax.axis_size("grp"), lax.axis_size("dp")
    w, g = place()
    span = length // nw
    rows = span // ng
    ff = down_weight.shape[1]
    part = -(-ff // (nw * 128)) * 128
    pad = nw * part - ff
    offset = w * span
    links = Links()

    weights = []
    (gains,) = links.gather_wid(norm_gains.reshape(2 * LAYERS, own))
    gains = gains.transpose(1, 0, 2).reshape(LAYERS, 2, D)
    for n in range(LAYERS):
        qkv_w, out_w = links.gather_wid(qkv_weight[n], out_weight[n])
        qkv_w = qkv_w.reshape(D, -1)
        out_w = out_w.transpose(1, 0, 2).reshape(QW, D)
        both = jnp.pad(gate_up[n], ((0, 0), (0, 0), (0, pad)))
        both = both.reshape(own, 2, nw, part).transpose(2, 1, 0, 3)
        both = links.swap("wid", both)
        gate_w = both[:, 0].reshape(D, part)
        up_w = both[:, 1].reshape(D, part)
        down_w = links.swap("wid", jnp.pad(down_weight[n], ((0, pad), (0, 0))).reshape(nw, part, own))
        down_w = down_w.transpose(1, 0, 2).reshape(part, D)
        weights.append((qkv_w, out_w, gate_w, up_w, down_w))

    both = jnp.stack([hidden_in[0], cotangent[0]]).reshape(2, nw, ng, rows, own)
    both = lax.dynamic_index_in_dim(both, g, 2, keepdims=False)
    both = both.transpose(1, 0, 2, 3).reshape(nw, 2 * rows, own)
    both = links.swap("wid", both).transpose(1, 0, 2).reshape(2, rows, D).astype(jnp.float32)
    h, grad = both[0], both[1]

    cosine_all, sine_all = rope_tables(doc_ids, offset, span)
    query_doc = lax.dynamic_slice_in_dim(doc_ids[0], offset, span, 0)
    query_place = offset + lax.iota(jnp.int32, span)
    key_place = lax.iota(jnp.int32, length)
    allowed = (key_place[None, :] <= query_place[:, None]) & (query_doc[:, None] == doc_ids[0][None, :])
    bias = jnp.where(allowed, 0.0, NEGATIVE).astype(jnp.float32)
    scale_row = jnp.concatenate(
        [jnp.full((QW,), HEAD_DIM ** (-0.5), jnp.float32), jnp.ones((2 * HEAD_DIM,), jnp.float32)]
    )

    stored = []
    for n in range(LAYERS):
        qkv_w, out_w, gate_w, up_w, down_w = weights[n]
        a1, r1 = normalize(h, gains[n, 0])
        a1 = links.swap("grp", a1, gather=True).reshape(span, D)
        p = dot(a1, qkv_w, NN) + qkv_bias[n]
        p = (rotate(p, cosine_all, sine_all) * scale_row).astype(LOW)
        q, kv = p[:, :QW], p[:, QW:]
        kv = links.swap("wid", kv, gather=True).reshape(length, 2 * HEAD_DIM)
        o = local_call(
            attend_kernel, jax.ShapeDtypeStruct(q.shape, LOW), (q, kv, bias), 4
        )
        y = dot(o, out_w, NN).astype(LOW).reshape(ng, rows, D)
        h1 = h + links.total("grp", y)
        a2, r2 = normalize(h1, gains[n, 1])
        a2 = links.gather_all(a2)
        gate = dot(a2, gate_w, NN)
        up = dot(a2, up_w, NN)
        m = (jax.nn.silu(gate) * up).astype(LOW)
        gate, up = gate.astype(LOW), up.astype(LOW)
        z = links.scatter_all(dot(m, down_w, NN).astype(LOW))
        stored.append((h, a1, r1, q, kv, o, h1, r2, a2, gate, up, m))
        h = h1 + z

    def to_width(values):
        pieces = values.astype(LOW).reshape(rows, nw, own).transpose(1, 0, 2)
        pieces = jnp.broadcast_to(pieces[:, None], (nw, ng, rows, own)).reshape(nw * ng, rows, own)
        return links.swap("all", pieces).reshape(1, length, own)

    hidden_out = to_width(h)

    grads = []
    small = []
    pending = ()
    for n in reversed(range(LAYERS)):
        qkv_w, out_w, gate_w, up_w, down_w = weights[n]
        h, a1, r1, q, kv, o, h1, r2, a2, gate, up, m = stored[n]
        gz = links.gather_all(grad.astype(LOW))
        dm = dot(gz, down_w, NT)
        gate, up = gate.astype(jnp.float32), up.astype(jnp.float32)
        sig = jax.nn.sigmoid(gate)
        dgate = (dm * up * sig * (1.0 + gate * (1.0 - sig))).astype(LOW)
        dup = (dm * (gate * sig)).astype(LOW)
        da2 = (dot(dgate, gate_w, NT) + dot(dup, up_w, NT)).astype(LOW)
        down_g = dot(m, gz, TN).astype(LOW)
        gate_g = jnp.stack([dot(a2, dgate, TN).astype(LOW), dot(a2, dup, TN).astype(LOW)])
        da2, down_g, gate_g, pending = lax.optimization_barrier((da2, down_g, gate_g, pending))
        if pending:
            grads.append(pending)
        da2 = links.scatter_all(da2)
        down_g = links.swap("wid", down_g.reshape(part, nw, own).transpose(1, 0, 2))
        down_g = down_g.reshape(nw * part, own)[:ff]
        down_g = lax.psum_scatter(down_g, "dp", scatter_dimension=0, tiled=True)
        gate_g = gate_g.reshape(2, nw, nd, own // nd, part).transpose(2, 1, 3, 0, 4)
        gate_g = gate_g.reshape(nd * nw * (own // nd), 2 * part)
        gate_g = lax.psum_scatter(gate_g, "dp", scatter_dimension=0, tiled=True)
        gate_g = links.swap("wid", gate_g.reshape(nw, own // nd, 2 * part))
        gate_g = gate_g.reshape(nw, own // nd, 2, part).transpose(1, 2, 0, 3)
        gate_g = gate_g.reshape(own // nd, 2, nw * part)[:, :, :ff]

        back, gain_two = normalize_back(h1, gains[n, 1], r2, da2)
        g1 = grad + back
        gy = links.swap("grp", g1.astype(LOW), gather=True).reshape(span, D)
        do = dot(gy, out_w, NT).astype(LOW)
        dq, dkv = local_call(
            attend_back_kernel,
            (jax.ShapeDtypeStruct(q.shape, jnp.float32), jax.ShapeDtypeStruct(kv.shape, LOW)),
            (q, kv, bias, do),
            8,
        )
        dkv = links.total("wid", dkv.reshape(nw, span, 2 * HEAD_DIM))
        dp = rotate(jnp.concatenate([dq, dkv], axis=1), cosine_all, -sine_all).astype(LOW)
        da1 = links.total("grp", dot(dp, qkv_w, NT).astype(LOW).reshape(ng, rows, D))
        back, gain_one = normalize_back(h, gains[n, 0], r1, da1)
        grad = g1 + back

        out_g = dot(o, gy, TN).astype(LOW)
        out_g = out_g.reshape(QW, nw, own).transpose(1, 0, 2).reshape(nw * QW, own)
        out_g = lax.psum_scatter(out_g, ("wid", "dp"), scatter_dimension=0, tiled=True)
        qkv_g = links.total("wid", dot(a1, dp, TN).astype(LOW).reshape(nw, own, -1)).astype(LOW)
        qkv_g = lax.psum_scatter(qkv_g, "dp", scatter_dimension=0, tiled=True)
        bias_g = jnp.sum(dp, axis=0, dtype=jnp.float32)
        bias_g = jnp.where(lax.iota(jnp.int32, ng)[:, None] == g, bias_g[None, :], 0.0).reshape(-1)
        small.append(jnp.concatenate([gain_one, gain_two, bias_g]))
        pending = (qkv_g, out_g, gate_g, down_g)

    grad, down_g, gate_g = lax.optimization_barrier((grad, pending[3], pending[2]))
    grads.append(pending[:2] + (gate_g, down_g))
    grads = [tuple(part_g.astype(jnp.float32) for part_g in member) for member in grads]
    input_grad = to_width(grad).astype(jnp.float32)
    grads, small = grads[::-1], small[::-1]
    small = jnp.stack(small)
    flat = small.reshape(-1, 128)
    flat = jnp.sum(links.swap("all", flat, gather=True), axis=0)
    small = jnp.sum(links.gather_dp(flat), axis=0).reshape(small.shape)
    at = lax.axis_index("dp")
    gain_g = small[:, : 2 * D].reshape(LAYERS, 2, D)
    gain_g = lax.dynamic_slice_in_dim(gain_g, w * own + at * (own // nd), own // nd, 2)
    bias_all = small[:, 2 * D :]
    width = bias_all.shape[1] // (ng * nd)
    bias_g = lax.dynamic_slice_in_dim(bias_all, (g * nd + at) * width, width, 1)
    return (
        hidden_out,
        input_grad,
        jnp.stack([member[0] for member in grads]),
        bias_g,
        jnp.stack([member[1] for member in grads]),
        jnp.stack([member[2] for member in grads]),
        jnp.stack([member[3] for member in grads]),
        gain_g,
    )


def solution(mesh):
    placed = (
        P("dp", None, "wid"),
        P("dp", None),
        P(None, "wid", "grp"),
        P(None, "grp"),
        P(None, "grp", "wid"),
        P(None, "wid", None, "grp"),
        P(None, "grp", "wid"),
        P(None, None, "wid"),
        P("dp", None, "wid"),
    )
    return jax.shard_map(
        per_device,
        mesh=mesh,
        in_specs=placed,
        out_specs=(
            P("dp", None, "wid"),
            P("dp", None, "wid"),
            P(None, ("wid", "dp"), "grp"),
            P(None, ("grp", "dp")),
            P(None, ("grp", "dp"), "wid"),
            P(None, ("wid", "dp"), None, "grp"),
            P(None, ("grp", "dp"), "wid"),
            P(None, None, ("wid", "dp")),
        ),
        check_vma=False,
    )
```
